32 devices in a mesh: parts: 2 (over x), freq: 16 (over z, y, core).
Axes of the slice: x: 2, y: 2, z: 4, core: 2. Of those that a mesh axis runs over, the one named last changes fastest.
Arguments:
- spectrum: float32 [32, 2, 2, 256, 256], P(('parts', 'freq')), parts along dimension 0, may hold values from -100 to 100
- blocks: bfloat16 [16, 2, 2, 1024, 1024], P('freq'), may hold values from -0.0625 to 0.0625
- scales: float32 [2, 4096], replicated, may hold values from 0.4 to 4
- iterate: float32 [32, 2, 2, 64, 1024], P(('parts', 'freq')), parts along dimension 0, may hold values from -3 to 3
Outputs:
- new_iterate: float32 [32, 2, 2, 64, 1024], P(('parts', 'freq')), parts along dimension 0
- new_residual: float32 [32, 2, 2, 256, 256], P(('parts', 'freq')), parts along dimension 0
The draws below stay inside these ranges and needn't reach their ends.
There are 2 independent parts, one for each index of `parts`. The reference program is written for one: setup_inputs(seed, part) draws one part's arguments, and reference() takes and returns one part's arrays. A program takes and returns all parts, laid end to end along the dimension named above; an argument that names none is the same for every part. Nothing has to cross between parts.
All inputs are finite; a program needn't handle non-finite values.
Results may differ from the reference program's by a relative error of at most 0.0027.
Values may be sent and summed in bfloat16 or wider, within the bound.
No kernel may reach another device: no remote copies, remote signals or barrier semaphores. Data moves between devices by JAX's collectives and lax.ppermute only.
A program may use at most 128 MiB of HBM per device.

```python
import math
import jax
import jax.numpy as jnp
from jax import lax

NR = 4096
NVS = 256
NFG = 2
NF = 2
BR = 1024
BC = 1024
SL = 256
VSL = 64
N_FREQ = 16


def draw_spectrum(key, part):
    noise_key, source_key, receiver_key = jax.random.split(key, 3)
    source_ramp = jnp.arange(NVS, dtype=jnp.float32) / float(NVS)
    source_gain = jnp.exp(source_ramp * math.log(3.0)) * jax.random.uniform(source_key, (NVS,), jnp.float32, 0.7, 1.3)
    device_ramp = jnp.arange(N_FREQ, dtype=jnp.float32) / float(N_FREQ)
    device_gain = jnp.exp(device_ramp * math.log(3.0))
    receiver_gain = jax.random.uniform(receiver_key, (N_FREQ, 1, 1, 1, SL), jnp.float32, 0.5, 2.0)
    shape = (N_FREQ, NFG, 2, NVS, SL)
    background = jnp.clip(jax.random.normal(noise_key, shape, jnp.float32), -4.0, 4.0)
    return background * source_gain[None, None, None, :, None] * device_gain[:, None, None, None, None] * receiver_gain


def block_levels(rng, dims, shards, least, top_value):
    def one(dim, parts):
        heights = jax.random.uniform(jax.random.fold_in(jax.random.fold_in(rng, 6), dim), (parts,), jnp.float32, least / len(shards), top_value / len(shards))
        return jnp.repeat(jnp.exp(heights), dims[dim] // parts).reshape((-1,) + (1,) * (len(dims) - dim - 1))

    loudness = one(*shards[0])
    for cut in shards[1:]:
        loudness = loudness * one(*cut)
    return loudness


def normal_values(stream_key, extent, width, limit, shards=(), held_as=jnp.bfloat16):
    factor_of = block_levels(stream_key, extent, shards, -0.22, 0.18) if shards else 1.0
    result = jax.random.normal(stream_key, extent, jnp.float32) * width * factor_of
    return jnp.minimum(jnp.maximum(result, -limit), limit).astype(held_as)


def setup_inputs(seed: int = 0, part: int = 0) -> dict:
    seeds = jax.random.split(jax.random.key(seed), 5)
    part_splits = jax.random.split(jax.random.fold_in(seeds[4], part), 5)
    spectrum = draw_spectrum(jax.random.fold_in(jax.random.fold_in(seeds[4], part), 71), part)
    blocks = normal_values(seeds[1], (N_FREQ, NFG, 2, BR, BC), (2 * NR) ** -0.5, 0.0625, ((0, 16),))
    scales = jnp.clip(jnp.exp(jax.random.uniform(seeds[2], (NF, NR), jnp.float32, math.log(0.4), math.log(4.0))), 0.4, 4.0)
    iterate = normal_values(part_splits[3], (N_FREQ, NFG, 2, VSL, BR), 0.5, 3.0, ((0, 16),), jnp.float32)
    return {"spectrum": spectrum, "blocks": blocks, "scales": scales, "iterate": iterate}


highest = lax.Precision.HIGHEST


def assemble_matrix(blocks):
    stacked = blocks.reshape(N_FREQ // 16, 4, 4, NFG, 2, BR, BC)
    stacked = jnp.transpose(stacked, (0, 3, 4, 2, 5, 1, 6))
    return stacked.reshape(NF, 2, NR, NR)


def unpack_iterate(iterate):
    stacked = iterate.reshape(N_FREQ // 16, 4, 4, NFG, 2, VSL, BR)
    stacked = jnp.transpose(stacked, (0, 3, 4, 1, 5, 2, 6))
    return stacked.reshape(NF, 2, NVS, NR)


def pack_iterate(field):
    stacked = field.reshape(N_FREQ // 16, NFG, 2, 4, VSL, 4, BR)
    stacked = jnp.transpose(stacked, (0, 3, 5, 1, 2, 4, 6))
    return stacked.reshape(N_FREQ, NFG, 2, VSL, BR)


def unpack_residual(packed):
    stacked = packed.reshape(N_FREQ // 16, 16, NFG, 2, NVS, SL)
    stacked = jnp.transpose(stacked, (0, 2, 3, 4, 1, 5))
    return stacked.reshape(NF, 2, NVS, NR)


def pack_residual(field):
    stacked = field.reshape(N_FREQ // 16, NFG, 2, NVS, 16, SL)
    stacked = jnp.transpose(stacked, (0, 4, 1, 2, 3, 5))
    return stacked.reshape(N_FREQ, NFG, 2, NVS, SL)


def rounded(values):
    return lax.optimization_barrier(values.astype(jnp.bfloat16)).astype(jnp.float32)


def complex_forward(operand, matrix):
    with_real = jnp.einsum('fcmk,fkn->fcmn', operand, matrix[:, 0], precision=highest)
    with_imag = jnp.einsum('fcmk,fkn->fcmn', operand, matrix[:, 1], precision=highest)
    return jnp.stack([with_real[:, 0] - with_imag[:, 1], with_imag[:, 0] + with_real[:, 1]], axis=1)


def complex_adjoint(residual_in, matrix):
    with_real = jnp.einsum('fcmn,fkn->fcmk', residual_in, matrix[:, 0], precision=highest)
    with_imag = jnp.einsum('fcmn,fkn->fcmk', residual_in, matrix[:, 1], precision=highest)
    return jnp.stack([with_real[:, 0] + with_imag[:, 1], with_real[:, 1] - with_imag[:, 0]], axis=1)


def reference(spectrum, blocks, scales, iterate):
    matrix = assemble_matrix(blocks).astype(jnp.float32)
    current = unpack_iterate(iterate)
    data_field = unpack_residual(spectrum)
    row_scale = scales[:, None, None, :]
    scaled = rounded(current * row_scale)
    image = complex_forward(scaled, matrix)
    residual = data_field - image
    descent = complex_adjoint(rounded(residual), matrix) * row_scale
    gamma = jnp.sum(descent * descent)
    lifted = rounded(descent * row_scale)
    curvature = complex_forward(lifted, matrix)
    bent = jnp.sum(curvature * curvature)
    step_size = gamma / bent
    new_iterate = pack_iterate(current + step_size * descent)
    new_residual = pack_residual(residual - step_size * curvature)
    return (new_iterate, new_residual)
```

```python
import jax
import jax.numpy as jnp
from jax import lax
from jax.sharding import PartitionSpec as P

ROWS = 4
COLS = 4
TEAM = ROWS * COLS
SPLIT = 1


def team_pairs(pairs):
    groups = lax.axis_size("freq") // TEAM
    return [(TEAM * g + a, TEAM * g + b) for g in range(groups) for a, b in pairs]


def along_columns(value, moves):
    pairs = [(ROWS * a + r, ROWS * b + r) for a, b in moves for r in range(ROWS)]
    return lax.ppermute(value, "freq", team_pairs(pairs))


def swap(value, bit):
    return lax.ppermute(value, "freq", team_pairs([(d, d ^ (1 << bit)) for d in range(TEAM)]))


def forward_product(field, matrix):
    real, imag = field[0], field[1]
    left = jnp.stack([jnp.stack([real, -imag], 1), jnp.stack([imag, real], 1)], 0)
    return lax.dot_general(
        left, matrix, (((2, 3), (0, 1)), ((), ())), preferred_element_type=jnp.float32
    )


def adjoint_product(field, matrix):
    real, imag = field[0], field[1]
    left = jnp.stack([jnp.stack([real, imag], 1), jnp.stack([imag, -real], 1)], 0)
    return lax.dot_general(
        left, matrix, (((2, 3), (0, 2)), ((), ())), preferred_element_type=jnp.float32
    )


def body(spectrum, blocks, scales, iterate):
    f32, bf16 = jnp.float32, jnp.bfloat16
    index = lax.axis_index("freq")
    core = index % 2
    y = index // 2 % 2
    row_block = index % ROWS
    col = index // ROWS % COLS
    group = index // TEAM
    matrix = blocks[0]
    current = iterate[0]
    data = spectrum[0]
    freqs, _, row_len, col_len = matrix.shape
    slab = current.shape[2]
    piece = slab // SPLIT
    part_len = col_len // ROWS
    own_scales = lax.dynamic_slice(
        scales, (group * freqs, row_block * row_len), (freqs, row_len)
    )
    is_hub = (col == 1) | (col == 2)

    def gather_columns(own):
        other = along_columns(own, [(0, 1), (1, 0), (2, 3), (3, 2)])
        odd = col % 2 == 1
        pair = jnp.where(odd, jnp.stack([other, own], 1), jnp.stack([own, other], 1))
        far_hub = along_columns(pair, [(1, 2), (2, 1)])
        far_end = along_columns(far_hub, [(1, 0), (2, 3)])
        far = jnp.where(is_hub, far_hub, far_end)
        both = jnp.where(
            col < 2, jnp.concatenate([pair, far], 1), jnp.concatenate([far, pair], 1)
        )
        return both.reshape(2, COLS * own.shape[1], own.shape[2])

    def scatter_rows(part):
        count = part.shape[1]
        pieces = part.reshape(2, count, 2, 2, part_len)
        sent = jnp.where(core == 0, pieces[:, :, :, 1], pieces[:, :, :, 0])
        kept = jnp.where(core == 0, pieces[:, :, :, 0], pieces[:, :, :, 1])
        half = kept + swap(sent, 0)
        sent = jnp.where(y == 0, half[:, :, 1], half[:, :, 0]).astype(bf16)
        kept = jnp.where(y == 0, half[:, :, 0], half[:, :, 1])
        return kept + swap(sent, 1).astype(f32)

    def gather_rows(own):
        other = swap(own, 1)
        pair = jnp.where(y == 0, jnp.stack([own, other], 2), jnp.stack([other, own], 2))
        far = swap(pair, 0)
        both = jnp.where(core == 0, jnp.stack([pair, far], 3), jnp.stack([far, pair], 3))
        return both.reshape(2, own.shape[1], col_len)

    def sum_columns(part):
        first = along_columns(part.astype(bf16), [(0, 1), (3, 2)]).astype(f32)
        second = along_columns((part + first).astype(bf16), [(1, 2), (2, 1)]).astype(f32)
        third = along_columns((part + second).astype(bf16), [(1, 0), (2, 3)]).astype(f32)
        return (part + first) + (second + third)

    chunks = [(f, h) for f in range(freqs) for h in range(SPLIT)]

    def data_rows(f, h):
        rows = data[f].reshape(2, COLS, SPLIT, piece, part_len)[:, :, h]
        return rows.reshape(2, COLS * piece, part_len)

    gathered = []
    for f, h in chunks:
        own = current[f, :, h * piece : (h + 1) * piece] * own_scales[f]
        gathered.append(gather_columns(own.astype(bf16)))
    residuals, descents, curvatures = [], [], []
    gamma, bent = 0.0, 0.0
    for (f, h), field in zip(chunks, gathered):
        image = scatter_rows(forward_product(field, matrix[f]))
        residual = data_rows(f, h) - image
        residuals.append(residual)
        summed = sum_columns(adjoint_product(gather_rows(residual.astype(bf16)), matrix[f]))
        descent = summed * own_scales[f]
        own = lax.dynamic_slice_in_dim(descent, col * piece, piece, 1)
        descents.append(own)
        gamma = gamma + jnp.sum(own * own)
        lifted = (descent * own_scales[f]).astype(bf16)
        curvature = scatter_rows(forward_product(lifted, matrix[f]))
        curvatures.append(curvature)
        bent = bent + jnp.sum(curvature * curvature)
    sums = jnp.stack([jnp.full((8, 128), gamma), jnp.full((8, 128), bent)])
    for bit in range(4):
        sums = sums + swap(sums, bit)
    step = sums[0, 0, 0] / sums[1, 0, 0]

    new_iterate, new_residual = [], []
    for f in range(freqs):
        mine = [n for n, (g, _) in enumerate(chunks) if g == f]
        descent = jnp.concatenate([descents[n] for n in mine], 1)
        new_iterate.append(current[f] + step * descent)
        fresh = [residuals[n] - step * curvatures[n] for n in mine]
        fresh = jnp.stack([r.reshape(2, COLS, piece, part_len) for r in fresh], 2)
        new_residual.append(fresh.reshape(2, COLS * slab, part_len))
    return (jnp.stack(new_iterate)[None], jnp.stack(new_residual)[None])


def solution(mesh):
    placed = P(("parts", "freq"), None, None, None, None)
    return jax.shard_map(
        body,
        mesh=mesh,
        in_specs=(placed, P("freq", None, None, None, None), P(), placed),
        out_specs=(placed, placed),
        check_vma=False,
    )
```

```python
import functools

import jax
import jax.numpy as jnp
from jax import lax
from jax.experimental import pallas as pl
from jax.experimental.pallas import tpu as pltpu
from jax.sharding import PartitionSpec as P

ROWS = 4
COLS = 4
TEAM = ROWS * COLS
SPLIT = 2
DIRECT = 4
LAG = {"R": 2, "I": 1, "D": 2, "H": 1, "A": 3, "B": 4, "C": 5, "K": 6, "J": 5}

f32, bf16 = jnp.float32, jnp.bfloat16
VMEM = pl.BlockSpec(memory_space=pltpu.VMEM)
SMEM = pl.BlockSpec(memory_space=pltpu.SMEM)
ANY = pl.BlockSpec(memory_space=pl.ANY)
shape = jax.ShapeDtypeStruct


def team_pairs(pairs):
    groups = lax.axis_size("freq") // TEAM
    return [(TEAM * g + a, TEAM * g + b) for g in range(groups) for a, b in pairs]


def along_columns(value, moves):
    pairs = [(ROWS * a + r, ROWS * b + r) for a, b in moves for r in range(ROWS)]
    return lax.ppermute(value, "freq", team_pairs(pairs))


def swap(value, bit):
    return lax.ppermute(value, "freq", team_pairs([(d, d ^ (1 << bit)) for d in range(TEAM)]))


NEIGHBOURS = [(0, 1), (1, 0), (2, 3), (3, 2)]
INWARD = [(0, 1), (3, 2)]
MIDDLE = [(1, 2), (2, 1)]
OUTWARD = [(1, 0), (2, 3)]


def product(left, right):
    return lax.dot_general(left, right, (((1,), (0,)), ((), ())), preferred_element_type=f32)


def product_transposed(left, right):
    return lax.dot_general(left, right, (((1,), (1,)), ((), ())), preferred_element_type=f32)


def multiply_columns(f, core, left, matrix, keep, *sends):
    count = left.shape[0] // 2
    width = keep.shape[-1]
    for which, outs in ((1 - core, sends), (core, [keep.at[half] for half in range(2)])):
        for half, out in enumerate(outs):
            cols = pl.ds(pl.multiple_of((2 * half + which) * width, width), width)
            with_real = product(left, matrix[f, 0, :, cols])
            with_imag = product(left, matrix[f, 1, :, cols])
            out[0] = with_real[:count] - with_imag[count:]
            out[1] = with_imag[:count] + with_real[count:]


def prepare_kernel(chunks, where, current, scales, *outs):
    core, y, col, group = where[0], where[1], where[2], where[3]
    freqs, _, _, depth = current.shape
    own_scales, outs = outs[0], outs[1:]
    cols = pl.ds(pl.multiple_of((2 * y + core) * depth, depth), depth)
    for f in range(freqs):
        own_scales[f : f + 1, :] = scales[pl.ds(group * freqs + f, 1), cols]
    for (f, start, size), out in zip(chunks, outs):
        for c in range(2):
            rows = current[f, c, start : start + size, :]
            out[c] = (rows * own_scales[f : f + 1, :]).astype(bf16)


def stack_kernel(where, own, other, out):
    out[0] = own[...]
    out[1] = other[...]


def image_kernel(f, direct, where, own, one, two, three, matrix, keep, *refs):
    core, col = where[0], where[2]
    *sends, left = refs
    left[:, col] = own[...]
    if direct:
        for k, ref in ((1, one), (2, two), (3, three)):
            left[:, lax.rem(col + COLS - k, COLS)] = ref[...]
    else:
        left[:, col + 1 - 2 * lax.rem(col, 2)] = one[...]
        low = (col < 2).astype(jnp.int32)
        for s in range(2):
            left[:, low * (2 + s) + (1 - low) * (1 - s)] = two[s] + three[s]
    rows = 2 * COLS * own.shape[1]
    multiply_columns(f, core, left[...].reshape(rows, own.shape[2]), matrix, keep, *sends)


def half_kernel(where, keep, lower, upper, low):
    for half, got in enumerate((lower, upper)):
        low[half] = (keep[half] + got[...]).astype(bf16)


def residual_kernel(f, start, size, where, keep, lower, upper, far, data, other_data, low, residual):
    y = where[1]
    slab = data.shape[2] // COLS
    for half, got in enumerate((lower, upper)):
        for source, mine in ((data, True), (other_data, False)):

            @pl.when((y == half) == mine)
            def _(half=half, got=got, source=source, mine=mine):
                for c in range(2):
                    for s in range(COLS):
                        rows = pl.ds(s * size, size)
                        image = (keep[half, c, rows] + got[c, rows]) + far[half, c, rows].astype(f32)
                        value = source[f, c, pl.ds(s * slab + start, size)] - image
                        low[half, c, rows] = value.astype(bf16)
                        if mine:
                            residual[c, rows] = value


def descent_kernel(f, where, own, other, matrix, low, part, left):
    core = where[0]
    count, width = own.shape[2], own.shape[3]
    for half in range(2):
        for which, ref in ((core, own), (1 - core, other)):
            cols = pl.ds(pl.multiple_of((2 * half + which) * width, width), width)
            left[:, cols] = ref[half].reshape(2 * count, width)
    depth = matrix.shape[2]
    tile = depth // 4
    for k in range(4):
        rows = pl.ds(k * tile, tile)
        with_real = product_transposed(left[...], matrix[f, 0, rows, :])
        with_imag = product_transposed(left[...], matrix[f, 1, rows, :])
        real = with_real[:count] + with_imag[count:]
        imag = with_real[count:] - with_imag[:count]
        part[0, :, rows], part[1, :, rows] = real, imag
        low[0, :, rows], low[1, :, rows] = real.astype(bf16), imag.astype(bf16)


def add_kernel(where, part, got, out):
    out[...] = (part[...] + got[...].astype(f32)).astype(bf16)


def curvature_kernel(f, where, part, first, second, third, scale, matrix, keep, *refs):
    core, col = where[0], where[2]
    *sends, own, left = refs
    count, depth = part.shape[1], part.shape[2]
    piece = own.shape[1]
    row_scale = scale[f : f + 1, :]

    def descent(c, rows):
        inner = part[c, rows] + first[c, rows].astype(f32)
        outer = second[c, rows].astype(f32) + third[c, rows].astype(f32)
        return (inner + outer) * row_scale

    for c in range(2):
        left[c] = (descent(c, pl.ds(0, count)) * row_scale).astype(bf16)
        own[c] = descent(c, pl.ds(pl.multiple_of(col * piece, piece), piece))
    multiply_columns(f, core, left[...].reshape(2 * count, depth), matrix, keep, *sends)


def bend_half_kernel(where, keep, lower, upper, low):
    for half, got in enumerate((lower, upper)):

        @pl.when(where[1] != half)
        def _(half=half, got=got):
            low[...] = (keep[half] + got[...]).astype(bf16)


def squares(value):
    return jnp.sum((value * value).reshape(-1, 8, 128), axis=0)


def bend_kernel(where, keep, lower, upper, far, own, sums, out_sums, curvature):
    for half, got in enumerate((lower, upper)):

        @pl.when(where[1] == half)
        def _(half=half, got=got):
            curvature[...] = (keep[half] + got[...]) + far[...].astype(f32)

    value = curvature[...]
    out_sums[0] = sums[0] + squares(own[...])
    out_sums[1] = sums[1] + squares(value)


def update_kernel(chunks, where, sums, current, *refs):
    n = len(chunks)
    descents, residuals, curvatures = refs[:n], refs[n : 2 * n], refs[2 * n : 3 * n]
    new_iterate, new_residual = refs[3 * n :]
    total = sums[...]
    step = jnp.sum(total[0], keepdims=True) / jnp.sum(total[1], keepdims=True)
    slab = new_residual.shape[3] // COLS
    for (f, start, size), descent, residual, curvature in zip(
        chunks, descents, residuals, curvatures
    ):
        for c in range(2):
            rows = pl.ds(start, size)
            new_iterate[0, f, c, rows] = current[f, c, rows] + step * descent[c]
            for s in range(COLS):
                rows = pl.ds(s * size, size)
                new_residual[0, f, c, pl.ds(s * slab + start, size)] = (
                    residual[c, rows] - step * curvature[c, rows]
                )


class Chain:
    def __init__(self, where):
        self.where = where
        self.last = None

    def __call__(self, kernel, name, out_shape, *operands, scratch=(), flops=0):
        token = [] if self.last is None else [self.last]

        def run(where, *refs):
            return kernel(where, *refs[len(token) :])

        results = pl.pallas_call(
            run,
            in_specs=[SMEM] + [ANY] * len(token) + [VMEM] * len(operands),
            out_specs=[VMEM] * len(out_shape),
            out_shape=out_shape,
            scratch_shapes=list(scratch),
            name=name,
            cost_estimate=pl.CostEstimate(
                flops=0, bytes_accessed=1024, transcendentals=0
            ),
            compiler_params=pltpu.CompilerParams(vmem_limit_bytes=32 << 20),
        )(self.where, *token, *operands)
        self.last = results[0]
        return results


def body(spectrum, blocks, scales, iterate):
    index = lax.axis_index("freq")
    where = jnp.stack([index % 2, index // 2 % 2, index // ROWS % COLS, index // TEAM])
    matrix, current, data = blocks[0], iterate[0], spectrum[0]
    freqs, _, row_len, col_len = matrix.shape
    slab, width = current.shape[2], data.shape[3]
    size = slab // SPLIT
    count = COLS * size
    flops = 8 * count * row_len * col_len
    chunks = [(f, h * size, size) for f in range(freqs) for h in range(SPLIT)]
    chain = Chain(where.astype(jnp.int32))

    other_data = swap(data, 1)
    own_scales, *owns = chain(
        functools.partial(prepare_kernel, chunks),
        "prepare",
        [shape((freqs, row_len), f32)] + [shape((2, s, row_len), bf16) for _, _, s in chunks],
        current,
        scales,
    )
    forward = [shape((2, 2, count, width), f32)] + [shape((2, count, width), f32)] * 2
    values = [{} for _ in chunks]
    totals = [jnp.zeros((2, 8, 128), f32)]

    for n, own in enumerate(owns):
        v = values[n]
        if n < DIRECT:
            shifts = [[(a, (a + k) % COLS) for a in range(COLS)] for k in (1, 2, 3)]
            v["x"] = (own, *(along_columns(own, moves) for moves in shifts))
        else:
            v["x"] = (own, along_columns(own, NEIGHBOURS))

    def step(kind, n):
        f, start, rows = chunks[n]
        v = values[n]
        if kind == "S" and n >= DIRECT:
            own, other = v["x"]
            (pair,) = chain(stack_kernel, "pair", [shape((2, *own.shape), bf16)], own, other)
            far_hub = along_columns(pair, MIDDLE)
            v["x"] = (own, other, far_hub, along_columns(far_hub, OUTWARD))
        elif kind == "I":
            v["keep"], *sends = chain(
                functools.partial(image_kernel, f, n < DIRECT),
                "image",
                forward,
                *v["x"],
                matrix,
                scratch=[pltpu.VMEM((2, COLS, rows, row_len), bf16)],
                flops=flops,
            )
            v["got"] = [swap(send, 0) for send in sends]
        elif kind == "H":
            (low,) = chain(half_kernel, "half", [shape((2, 2, count, width), bf16)], v["keep"], *v["got"])
            v["far"] = swap(low, 1)
        elif kind == "R":
            v["low"], v["residual"] = chain(
                functools.partial(residual_kernel, f, start, rows),
                "residual",
                [shape((2, 2, count, width), bf16), shape((2, count, width), f32)],
                v["keep"],
                *v["got"],
                v["far"],
                data,
                other_data,
            )
            v["other_low"] = swap(v["low"], 0)
        elif kind == "D":
            low, v["part"] = chain(
                functools.partial(descent_kernel, f),
                "descent",
                [shape((2, count, row_len), bf16), shape((2, count, row_len), f32)],
                v["low"],
                v["other_low"],
                matrix,
                scratch=[pltpu.VMEM((2 * count, col_len), bf16)],
                flops=flops,
            )
            v["first"] = along_columns(low, INWARD)
        elif kind in "AB":
            name, source, moves = (
                ("second", "first", MIDDLE) if kind == "A" else ("third", "second", OUTWARD)
            )
            (low,) = chain(add_kernel, "add", [shape((2, count, row_len), bf16)], v["part"], v[source])
            v[name] = along_columns(low, moves)
        elif kind == "C":
            v["keep"], *sends, v["own"] = chain(
                functools.partial(curvature_kernel, f),
                "curvature",
                forward + [shape((2, rows, row_len), f32)],
                v["part"],
                v["first"],
                v["second"],
                v["third"],
                own_scales,
                matrix,
                scratch=[pltpu.VMEM((2, count, row_len), bf16)],
                flops=flops,
            )
            v["got"] = [swap(send, 0) for send in sends]
        elif kind == "J":
            (low,) = chain(
                bend_half_kernel, "bend_half", [shape((2, count, width), bf16)], v["keep"], *v["got"]
            )
            v["far"] = swap(low, 1)
        elif kind == "K":
            totals[0], v["curvature"] = chain(
                bend_kernel,
                "bend",
                [shape((2, 8, 128), f32), shape((2, count, width), f32)],
                v["keep"],
                *v["got"],
                v["far"],
                v["own"],
                totals[0],
            )

    for turn in range(max(LAG.values()) + len(chunks)):
        for kind, lag in LAG.items():
            if 0 <= turn - lag < len(chunks):
                step(kind, turn - lag)

    sums = totals[0]
    for bit in range(4):
        sums = sums + swap(sums, bit)
    return chain(
        functools.partial(update_kernel, chunks),
        "update",
        [shape(iterate.shape, f32), shape(spectrum.shape, f32)],
        sums,
        current,
        *(v[name] for name in ("own", "residual", "curvature") for v in values),
    )


def solution(mesh):
    placed = P(("parts", "freq"), None, None, None, None)
    return jax.shard_map(
        body,
        mesh=mesh,
        in_specs=(placed, P("freq", None, None, None, None), P(), placed),
        out_specs=(placed, placed),
        check_vma=False,
    )
```

```python
import functools

import jax
import jax.numpy as jnp
from jax import lax
from jax.experimental import pallas as pl
from jax.experimental.pallas import tpu as pltpu
from jax.sharding import PartitionSpec as P

ROWS = 4
COLS = 4
TEAM = ROWS * COLS
SIZES = ((2, 2), (2, 2))
GROUPS = ((0,), (1,), (2,), (3,))
LAG = {"I": 1, "R": 2, "H": 1, "D": 2, "A": 3, "B": 4, "C": 5, "J": 5, "K": 7}

CORE = 2

f32, bf16 = jnp.float32, jnp.bfloat16
VMEM = pl.BlockSpec(memory_space=pltpu.VMEM)
SMEM = pl.BlockSpec(memory_space=pltpu.SMEM)
ANY = pl.BlockSpec(memory_space=pl.ANY)
HBM = pl.BlockSpec(memory_space=pltpu.HBM)
shape = jax.ShapeDtypeStruct


def team_pairs(pairs):
    groups = lax.axis_size("freq") // TEAM
    return [(TEAM * g + a, TEAM * g + b) for g in range(groups) for a, b in pairs]


def along_columns(value, moves):
    pairs = [(ROWS * a + r, ROWS * b + r) for a, b in moves for r in range(ROWS)]
    return lax.ppermute(value, "freq", team_pairs(pairs))


def swap(value, bit):
    return lax.ppermute(value, "freq", team_pairs([(d, d ^ (1 << bit)) for d in range(TEAM)]))


INWARD = [(0, 1), (3, 2)]
MIDDLE = [(1, 2), (2, 1)]
OUTWARD = [(1, 0), (2, 3)]
SHIFTS = [[(a, (a + k) % COLS) for a in range(COLS)] for k in range(1, COLS)]


def product(left, right):
    return lax.dot_general(left, right, (((1,), (0,)), ((), ())), preferred_element_type=f32)


def product_transposed(left, right):
    return lax.dot_general(left, right, (((1,), (1,)), ((), ())), preferred_element_type=f32)


def slab_of(refs, n):
    each = 4 // len(refs)
    return refs[n // each].at[n % each]


def multiply_columns(core, left, matrix, keep, *sends):
    count = left.shape[0] // 2
    width = keep.shape[3]
    away = [slab_of(sends, n) for n in range(4)]
    for which, outs in ((1 - core, away), (core, [keep.at[n // 2, n % 2] for n in range(4)])):
        for half in range(2):
            real, imag = outs[2 * half : 2 * half + 2]
            cols = pl.ds(pl.multiple_of((2 * half + which) * width, width), width)
            with_real = product(left, matrix[0, :, cols])
            with_imag = product(left, matrix[1, :, cols])
            real[...] = with_real[:count] - with_imag[count:]
            imag[...] = with_imag[:count] + with_real[count:]


def load_kernel(where, matrix_hbm, data_hbm, *refs):
    freqs = matrix_hbm.shape[0]
    datas, matrices, sems = refs[-1 - 2 * freqs : -1 - freqs], refs[-1 - freqs : -1], refs[-1]
    pairs = [(data_hbm.at[f], data) for f, data in enumerate(datas)]
    pairs += [(matrix_hbm.at[f], matrix) for f, matrix in enumerate(matrices)]
    copies = [
        pltpu.make_async_copy(source, target, sems.at[n]) for n, (source, target) in enumerate(pairs)
    ]
    for copy in copies:
        copy.start()
    for copy in copies:
        copy.wait()


def image_kernel(start, where, *refs):
    core, col = where[0], where[2]
    fields, (matrix, keep, *sends, left) = refs[:COLS], refs[COLS:]
    for k, field in enumerate(fields):
        left[:, lax.rem(col + COLS - k, COLS)] = field[:, start : start + left.shape[2]]
    rows = 2 * COLS * left.shape[2]
    multiply_columns(core, left[...].reshape(rows, left.shape[3]), matrix, keep, *sends)


def half_kernel(where, keep, *refs):
    *got, low = refs
    for n in range(4):
        low[n // 2, n % 2] = (keep[n // 2, n % 2] + slab_of(got, n)[...]).astype(bf16)


def residual_kernel(start, size, where, keep, *refs):
    *got, far, data, other_data, low, residual = refs
    y = where[1]
    slab = data.shape[1] // COLS
    for half in range(2):
        for source, mine in ((data, True), (other_data, False)):

            @pl.when((y == half) == mine)
            def _(half=half, source=source, mine=mine):
                for c in range(2):
                    for s in range(COLS):
                        rows = pl.ds(s * size, size)
                        image = (keep[half, c, rows] + slab_of(got, 2 * half + c)[rows]) + far[half, c, rows].astype(f32)
                        value = source[c, pl.ds(s * slab + start, size)] - image
                        low[half, c, rows] = value.astype(bf16)
                        if mine:
                            residual[c, rows] = value


def descent_kernel(where, own, other, matrix, low, part, left):
    core = where[0]
    count, width = own.shape[2], own.shape[3]
    for half in range(2):
        for which, ref in ((core, own), (1 - core, other)):
            cols = pl.ds(pl.multiple_of((2 * half + which) * width, width), width)
            left[:, cols] = ref[half].reshape(2 * count, width)
    depth = matrix.shape[1]
    tile = depth // 4
    for k in range(4):
        rows = pl.ds(k * tile, tile)
        with_real = product_transposed(left[...], matrix[0, rows, :])
        with_imag = product_transposed(left[...], matrix[1, rows, :])
        real = with_real[:count] + with_imag[count:]
        imag = with_real[count:] - with_imag[:count]
        part[0, :, rows], part[1, :, rows] = real, imag
        low[0, :, rows], low[1, :, rows] = real.astype(bf16), imag.astype(bf16)


def add_kernel(where, part, got, out):
    out[...] = (part[...] + got[...].astype(f32)).astype(bf16)


def curvature_kernel(f, where, part, first, second, third, scale, matrix, keep, *refs):
    core, col = where[0], where[2]
    *sends, own, left = refs
    count, depth = part.shape[1], part.shape[2]
    piece = own.shape[1]
    row_scale = scale[f : f + 1, :]

    def descent(c, rows):
        inner = part[c, rows] + first[c, rows].astype(f32)
        outer = second[c, rows].astype(f32) + third[c, rows].astype(f32)
        return (inner + outer) * row_scale

    for c in range(2):
        left[c] = (descent(c, pl.ds(0, count)) * row_scale).astype(bf16)
        own[c] = descent(c, pl.ds(pl.multiple_of(col * piece, piece), piece))
    multiply_columns(core, left[...].reshape(2 * count, depth), matrix, keep, *sends)


def bend_half_kernel(where, keep, *refs):
    *got, low = refs
    for half in range(2):

        @pl.when(where[1] != half)
        def _(half=half):
            for c in range(2):
                low[c] = (keep[half, c] + slab_of(got, 2 * half + c)[...]).astype(bf16)


def squares(value):
    return jnp.sum((value * value).reshape(-1, 8, 128), axis=0)


def bend_kernel(where, keep, *refs):
    *got, far, own, sums, out_sums, curvature = refs
    for half in range(2):

        @pl.when(where[1] == half)
        def _(half=half):
            for c in range(2):
                curvature[c] = (keep[half, c] + slab_of(got, 2 * half + c)[...]) + far[c].astype(f32)

    value = curvature[...]
    out_sums[0] = sums[0] + squares(own[...])
    out_sums[1] = sums[1] + squares(value)


def spread_kernel(where, sums, out):
    rows = [jnp.sum(sums[n], axis=0, keepdims=True) for n in range(2)]
    out[...] = jnp.broadcast_to(jnp.concatenate(rows * 4, axis=0)[None], out.shape)


def update_kernel(chunks, where, sums, current, *refs):
    n = len(chunks)
    descents, residuals, curvatures = refs[:n], refs[n : 2 * n], refs[2 * n : 3 * n]
    new_iterate, new_residual = refs[3 * n :]
    total = jnp.sum(sums[...], axis=0)
    step = jnp.sum(total[:1], keepdims=True) / jnp.sum(total[1:2], keepdims=True)
    slab = new_residual.shape[3] // COLS
    for (f, start, size), descent, residual, curvature in zip(
        chunks, descents, residuals, curvatures
    ):
        for c in range(2):
            rows = pl.ds(start, size)
            new_iterate[0, f, c, rows] = current[f, c, rows] + step * descent[c]
            for s in range(COLS):
                rows = pl.ds(s * size, size)
                new_residual[0, f, c, pl.ds(s * slab + start, size)] = (
                    residual[c, rows] - step * curvature[c, rows]
                )


class Chain:
    def __init__(self, where):
        self.where = where
        self.last = None

    def __call__(self, kernel, name, out_shape, *operands, scratch=(), flops=0, specs=None):
        token = [] if self.last is None else [self.last]

        def run(where, *refs):
            return kernel(where, *refs[len(token) :])

        results = pl.pallas_call(
            run,
            in_specs=[SMEM] + [ANY] * len(token) + (specs or [VMEM] * len(operands)),
            out_specs=[VMEM] * len(out_shape),
            out_shape=out_shape,
            scratch_shapes=list(scratch),
            name=name,
            cost_estimate=pl.CostEstimate(
                flops=0, bytes_accessed=1024, transcendentals=0
            ),
            compiler_params=pltpu.CompilerParams(vmem_limit_bytes=32 << 20),
        )(self.where, *token, *operands)
        self.last = results[0]
        return results


def body(spectrum, blocks, scales, iterate):
    index = lax.axis_index("freq")
    where = jnp.stack([index % 2, index // 2 % 2, index // ROWS % COLS, index // TEAM])
    matrix, current, data = blocks[0], iterate[0], spectrum[0]
    freqs, _, row_len, col_len = matrix.shape
    slab, width = current.shape[2], data.shape[3]
    chunks = []
    for f in range(freqs):
        sizes = [slab // 4 * part for part in SIZES[f]]
        chunks += [(f, sum(sizes[:h]), size) for h, size in enumerate(sizes)]
    sent = [[chunks[n] for n in members] for members in GROUPS]
    chain = Chain(where.astype(jnp.int32))

    own_scales = lax.dynamic_slice(
        scales, (index // TEAM * freqs, index % ROWS * row_len), (freqs, row_len)
    )
    owns = [
        jnp.concatenate(
            [current[f, :, start : start + rows] * own_scales[f] for f, start, rows in members], 1
        ).astype(bf16)
        for members in sent
    ]
    staged = chain(
        load_kernel,
        "load",
        [shape(data.shape[1:], f32)] * freqs + [shape(matrix.shape[1:], bf16)] * freqs,
        matrix,
        data,
        *owns,
        specs=[HBM] * 2 + [ANY] * len(owns),
        scratch=[pltpu.SemaphoreType.DMA((2 * freqs,))],
    )
    data, matrices = staged[:freqs], staged[freqs:]
    other_data = [swap(rows, 1) for rows in data]
    values = [{} for _ in chunks]
    totals = [jnp.zeros((2, 8, 128), f32)]

    for members, own in zip(GROUPS, owns):
        gathered = (own, *(along_columns(own, moves) for moves in SHIFTS))
        place = 0
        for n in members:
            values[n]["x"], values[n]["start"] = gathered, place
            place += chunks[n][2]

    def step(kind, n):
        f, start, rows = chunks[n]
        v = values[n]
        count = COLS * rows
        flops = 8 * count * row_len * col_len
        forward = [shape((2, 2, count, width), f32)] + [shape((4 // CORE, count, width), f32)] * CORE
        if kind == "I":
            v["keep"], *sends = chain(
                functools.partial(image_kernel, v["start"]),
                "image",
                forward,
                *v["x"],
                matrices[f],
                scratch=[pltpu.VMEM((2, COLS, rows, row_len), bf16)],
                flops=flops,
            )
            v["got"] = [swap(send, 0) for send in sends]
        elif kind == "H":
            (low,) = chain(half_kernel, "half", [shape((2, 2, count, width), bf16)], v["keep"], *v["got"])
            v["far"] = swap(low, 1)
        elif kind == "R":
            v["low"], v["residual"] = chain(
                functools.partial(residual_kernel, start, rows),
                "residual",
                [shape((2, 2, count, width), bf16), shape((2, count, width), f32)],
                v["keep"],
                *v["got"],
                v["far"],
                data[f],
                other_data[f],
            )
            v["other_low"] = swap(v["low"], 0)
        elif kind == "D":
            low, v["part"] = chain(
                descent_kernel,
                "descent",
                [shape((2, count, row_len), bf16), shape((2, count, row_len), f32)],
                v["low"],
                v["other_low"],
                matrices[f],
                scratch=[pltpu.VMEM((2 * count, col_len), bf16)],
                flops=flops,
            )
            v["first"] = along_columns(low, INWARD)
        elif kind in "AB":
            name, source, moves = (
                ("second", "first", MIDDLE) if kind == "A" else ("third", "second", OUTWARD)
            )
            (low,) = chain(add_kernel, "add", [shape((2, count, row_len), bf16)], v["part"], v[source])
            v[name] = along_columns(low, moves)
        elif kind == "C":
            v["keep"], *sends, v["own"] = chain(
                functools.partial(curvature_kernel, f),
                "curvature",
                forward + [shape((2, rows, row_len), f32)],
                v["part"],
                v["first"],
                v["second"],
                v["third"],
                own_scales,
                matrices[f],
                scratch=[pltpu.VMEM((2, count, row_len), bf16)],
                flops=flops,
            )
            v["got"] = [swap(send, 0) for send in sends]
        elif kind == "J":
            (low,) = chain(
                bend_half_kernel, "bend_half", [shape((2, count, width), bf16)], v["keep"], *v["got"]
            )
            v["far"] = swap(low, 1)
        elif kind == "K":
            totals[0], v["curvature"] = chain(
                bend_kernel,
                "bend",
                [shape((2, 8, 128), f32), shape((2, count, width), f32)],
                v["keep"],
                *v["got"],
                v["far"],
                v["own"],
                totals[0],
            )

    for turn in range(max(LAG.values()) + len(chunks)):
        for kind, lag in LAG.items():
            if 0 <= turn - lag < len(chunks):
                step(kind, turn - lag)

    (sums,) = chain(spread_kernel, "spread", [shape((TEAM, 8, 128), f32)], totals[0])
    teams = lax.axis_size("freq") // TEAM
    members = [[TEAM * g + d for d in range(TEAM)] for g in range(teams)]
    sums = lax.all_to_all(sums, "freq", 0, 0, axis_index_groups=members)
    return chain(
        functools.partial(update_kernel, chunks),
        "update",
        [shape(iterate.shape, f32), shape(spectrum.shape, f32)],
        sums,
        current,
        *(v[name] for name in ("own", "residual", "curvature") for v in values),
    )


def solution(mesh):
    placed = P(("parts", "freq"), None, None, None, None)
    return jax.shard_map(
        body,
        mesh=mesh,
        in_specs=(placed, P("freq", None, None, None, None), P(), placed),
        out_specs=(placed, placed),
        check_vma=False,
    )
```

```python
import functools

import jax
import jax.numpy as jnp
from jax import lax
from jax.experimental import pallas as pl
from jax.experimental.pallas import tpu as pltpu
from jax.sharding import PartitionSpec as P

ROWS = 4
COLS = 4
TEAM = ROWS * COLS
SIZES = ((2, 2), (2, 2))
GROUPS = ((0,), (1,), (2,), (3,))
LAG = {"I": 1, "R": 2, "H": 1, "D": 2, "A": 3, "B": 4, "K": 7, "C": 5, "J": 5}

CORE = 2

f32, bf16 = jnp.float32, jnp.bfloat16
VMEM = pl.BlockSpec(memory_space=pltpu.VMEM)
SMEM = pl.BlockSpec(memory_space=pltpu.SMEM)
ANY = pl.BlockSpec(memory_space=pl.ANY)
HBM = pl.BlockSpec(memory_space=pltpu.HBM)
shape = jax.ShapeDtypeStruct


def team_pairs(pairs):
    groups = lax.axis_size("freq") // TEAM
    return [(TEAM * g + a, TEAM * g + b) for g in range(groups) for a, b in pairs]


def along_columns(value, moves):
    pairs = [(ROWS * a + r, ROWS * b + r) for a, b in moves for r in range(ROWS)]
    return lax.ppermute(value, "freq", team_pairs(pairs))


def swap(value, bit):
    return lax.ppermute(value, "freq", team_pairs([(d, d ^ (1 << bit)) for d in range(TEAM)]))


INWARD = [(0, 1), (3, 2)]
MIDDLE = [(1, 2), (2, 1)]
OUTWARD = [(1, 0), (2, 3)]
SHIFTS = [[(a, (a + k) % COLS) for a in range(COLS)] for k in range(1, COLS)]


def product(left, right):
    return lax.dot_general(left, right, (((1,), (0,)), ((), ())), preferred_element_type=f32)


def product_transposed(left, right):
    return lax.dot_general(left, right, (((1,), (1,)), ((), ())), preferred_element_type=f32)


def slab_of(refs, n):
    each = 4 // len(refs)
    return refs[n // each].at[n % each]


def multiply_columns(core, left, matrix, keep, *sends):
    count = left.shape[0] // 2
    width = keep.shape[3]
    away = [slab_of(sends, n) for n in range(4)]
    for which, outs in ((1 - core, away), (core, [keep.at[n // 2, n % 2] for n in range(4)])):
        for half in range(2):
            real, imag = outs[2 * half : 2 * half + 2]
            cols = pl.ds(pl.multiple_of((2 * half + which) * width, width), width)
            with_real = product(left, matrix[0, :, cols])
            with_imag = product(left, matrix[1, :, cols])
            real[...] = with_real[:count] - with_imag[count:]
            imag[...] = with_imag[:count] + with_real[count:]


def load_kernel(groups, where, matrix_hbm, data_hbm, _, current, scale, *refs):
    freqs = matrix_hbm.shape[0]
    datas, matrices, sems = refs[:freqs], refs[freqs : 2 * freqs], refs[-1]
    pairs = [(data_hbm.at[f], data) for f, data in enumerate(datas)]
    pairs += [(matrix_hbm.at[f], matrix) for f, matrix in enumerate(matrices)]
    copies = [
        pltpu.make_async_copy(source, target, sems.at[n]) for n, (source, target) in enumerate(pairs)
    ]
    for copy in copies:
        copy.start()
    for members, out in zip(groups, refs[2 * freqs : -1]):
        place = 0
        for f, start, size in members:
            for c in range(2):
                rows = current[f, c, start : start + size, :]
                out[c, place : place + size] = (rows * scale[f : f + 1, :]).astype(bf16)
            place += size
    for copy in copies:
        copy.wait()


def image_kernel(start, where, *refs):
    core, col = where[0], where[2]
    fields, (matrix, keep, *sends, left) = refs[:COLS], refs[COLS:]
    for k, field in enumerate(fields):
        left[:, lax.rem(col + COLS - k, COLS)] = field[:, start : start + left.shape[2]]
    rows = 2 * COLS * left.shape[2]
    multiply_columns(core, left[...].reshape(rows, left.shape[3]), matrix, keep, *sends)


def half_kernel(where, keep, *refs):
    *got, low = refs
    for n in range(4):
        low[n // 2, n % 2] = (keep[n // 2, n % 2] + slab_of(got, n)[...]).astype(bf16)


def residual_kernel(start, size, where, keep, *refs):
    *got, far, data, other_data, low, residual = refs
    y = where[1]
    slab = data.shape[1] // COLS
    for half in range(2):
        for source, mine in ((data, True), (other_data, False)):

            @pl.when((y == half) == mine)
            def _(half=half, source=source, mine=mine):
                for c in range(2):
                    for s in range(COLS):
                        rows = pl.ds(s * size, size)
                        image = (keep[half, c, rows] + slab_of(got, 2 * half + c)[rows]) + far[half, c, rows].astype(f32)
                        value = source[c, pl.ds(s * slab + start, size)] - image
                        low[half, c, rows] = value.astype(bf16)
                        if mine:
                            residual[c, rows] = value


def descent_kernel(where, own, other, matrix, low, part, left):
    core = where[0]
    count, width = own.shape[2], own.shape[3]
    for half in range(2):
        for which, ref in ((core, own), (1 - core, other)):
            cols = pl.ds(pl.multiple_of((2 * half + which) * width, width), width)
            left[:, cols] = ref[half].reshape(2 * count, width)
    depth = matrix.shape[1]
    tile = depth // 4
    for k in range(4):
        rows = pl.ds(k * tile, tile)
        with_real = product_transposed(left[...], matrix[0, rows, :])
        with_imag = product_transposed(left[...], matrix[1, rows, :])
        real = with_real[:count] + with_imag[count:]
        imag = with_real[count:] - with_imag[:count]
        part[0, :, rows], part[1, :, rows] = real, imag
        low[0, :, rows], low[1, :, rows] = real.astype(bf16), imag.astype(bf16)


def add_kernel(where, part, got, out):
    out[...] = (part[...] + got[...].astype(f32)).astype(bf16)


def curvature_kernel(f, where, part, first, second, third, scale, matrix, keep, *refs):
    core, col = where[0], where[2]
    *sends, own, left = refs
    count, depth = part.shape[1], part.shape[2]
    piece = own.shape[1]
    row_scale = scale[f : f + 1, :]

    def descent(c, rows):
        inner = part[c, rows] + first[c, rows].astype(f32)
        outer = second[c, rows].astype(f32) + third[c, rows].astype(f32)
        return (inner + outer) * row_scale

    for c in range(2):
        left[c] = (descent(c, pl.ds(0, count)) * row_scale).astype(bf16)
        own[c] = descent(c, pl.ds(pl.multiple_of(col * piece, piece), piece))
    multiply_columns(core, left[...].reshape(2 * count, depth), matrix, keep, *sends)


def bend_half_kernel(where, keep, *refs):
    *got, low = refs
    for half in range(2):

        @pl.when(where[1] != half)
        def _(half=half):
            for c in range(2):
                low[c] = (keep[half, c] + slab_of(got, 2 * half + c)[...]).astype(bf16)


def squares(value):
    return jnp.sum((value * value).reshape(-1, 8, 128), axis=0)


def bend_kernel(where, keep, *refs):
    *got, far, own, sums, out_sums, curvature = refs
    for half in range(2):

        @pl.when(where[1] == half)
        def _(half=half):
            for c in range(2):
                curvature[c] = (keep[half, c] + slab_of(got, 2 * half + c)[...]) + far[c].astype(f32)

    value = curvature[...]
    out_sums[0] = sums[0] + squares(own[...])
    out_sums[1] = sums[1] + squares(value)


def spread_kernel(where, *refs):
    *refs, out = refs
    bend_kernel(where, *refs)
    gamma, bent = (jnp.sum(refs[-2][n], keepdims=True) for n in range(2))
    lane = lax.broadcasted_iota(jnp.int32, out.shape, 1)
    out[...] = jnp.where(lane < out.shape[1] // 2, gamma, bent)


def update_kernel(chunks, where, sums, current, *refs):
    n = len(chunks)
    descents, residuals, curvatures = refs[:n], refs[n : 2 * n], refs[2 * n : 3 * n]
    new_iterate, new_residual = refs[3 * n :]
    total = jnp.sum(sums[...], axis=0, keepdims=True)
    middle = total.shape[1] // 2
    step = total[:, :1] / total[:, middle : middle + 1]
    slab = new_residual.shape[3] // COLS
    for (f, start, size), descent, residual, curvature in zip(
        chunks, descents, residuals, curvatures
    ):
        for c in range(2):
            rows = pl.ds(start, size)
            new_iterate[0, f, c, rows] = current[f, c, rows] + step * descent[c]
            for s in range(COLS):
                rows = pl.ds(s * size, size)
                new_residual[0, f, c, pl.ds(s * slab + start, size)] = (
                    residual[c, rows] - step * curvature[c, rows]
                )


class Chain:
    def __init__(self, where):
        self.where = where
        self.last = None

    def __call__(self, kernel, name, out_shape, *operands, scratch=(), flops=0, specs=None):
        token = [] if self.last is None else [self.last]

        def run(where, *refs):
            return kernel(where, *refs[len(token) :])

        results = pl.pallas_call(
            run,
            in_specs=[SMEM] + [ANY] * len(token) + (specs or [VMEM] * len(operands)),
            out_specs=[VMEM] * len(out_shape),
            out_shape=out_shape,
            scratch_shapes=list(scratch),
            name=name,
            cost_estimate=pl.CostEstimate(
                flops=0, bytes_accessed=1024, transcendentals=0
            ),
            compiler_params=pltpu.CompilerParams(vmem_limit_bytes=32 << 20),
        )(self.where, *token, *operands)
        self.last = results[0]
        return results


def body(spectrum, blocks, scales, iterate):
    index = lax.axis_index("freq")
    where = jnp.stack([index % 2, index // 2 % 2, index // ROWS % COLS, index // TEAM])
    matrix, current, data = blocks[0], iterate[0], spectrum[0]
    freqs, _, row_len, col_len = matrix.shape
    slab, width = current.shape[2], data.shape[3]
    chunks = []
    for f in range(freqs):
        sizes = [slab // 4 * part for part in SIZES[f]]
        chunks += [(f, sum(sizes[:h]), size) for h, size in enumerate(sizes)]
    sent = [[chunks[n] for n in members] for members in GROUPS]
    chain = Chain(where.astype(jnp.int32))

    own_scales = lax.dynamic_slice(
        scales, (index // TEAM * freqs, index % ROWS * row_len), (freqs, row_len)
    )
    f, start, rows = sent[0][0]
    owns = [(current[f, :, start : start + rows] * own_scales[f]).astype(bf16)]
    staged = chain(
        functools.partial(load_kernel, sent[1:]),
        "load",
        [shape(data.shape[1:], f32)] * freqs
        + [shape(matrix.shape[1:], bf16)] * freqs
        + [shape((2, sum(c[2] for c in members), row_len), bf16) for members in sent[1:]],
        matrix,
        data,
        owns[0],
        current,
        own_scales,
        specs=[HBM] * 2 + [ANY] + [VMEM] * 2,
        scratch=[pltpu.SemaphoreType.DMA((2 * freqs,))],
    )
    data, matrices = staged[:freqs], staged[freqs : 2 * freqs]
    owns += staged[2 * freqs :]
    other_data = [swap(rows, 1) for rows in data]
    values = [{} for _ in chunks]
    totals, spread = [jnp.zeros((2, 8, 128), f32)], []

    for members, own in zip(GROUPS, owns):
        gathered = (own, *(along_columns(own, moves) for moves in SHIFTS))
        place = 0
        for n in members:
            values[n]["x"], values[n]["start"] = gathered, place
            place += chunks[n][2]

    def step(kind, n):
        f, start, rows = chunks[n]
        v = values[n]
        count = COLS * rows
        flops = 8 * count * row_len * col_len
        forward = [shape((2, 2, count, width), f32)] + [shape((4 // CORE, count, width), f32)] * CORE
        if kind == "I":
            v["keep"], *sends = chain(
                functools.partial(image_kernel, v["start"]),
                "image",
                forward,
                *v["x"],
                matrices[f],
                scratch=[pltpu.VMEM((2, COLS, rows, row_len), bf16)],
                flops=flops,
            )
            v["got"] = [swap(send, 0) for send in sends]
        elif kind == "H":
            (low,) = chain(half_kernel, "half", [shape((2, 2, count, width), bf16)], v["keep"], *v["got"])
            v["far"] = swap(low, 1)
        elif kind == "R":
            v["low"], v["residual"] = chain(
                functools.partial(residual_kernel, start, rows),
                "residual",
                [shape((2, 2, count, width), bf16), shape((2, count, width), f32)],
                v["keep"],
                *v["got"],
                v["far"],
                data[f],
                other_data[f],
            )
            v["other_low"] = swap(v["low"], 0)
        elif kind == "D":
            low, v["part"] = chain(
                descent_kernel,
                "descent",
                [shape((2, count, row_len), bf16), shape((2, count, row_len), f32)],
                v["low"],
                v["other_low"],
                matrices[f],
                scratch=[pltpu.VMEM((2 * count, col_len), bf16)],
                flops=flops,
            )
            v["first"] = along_columns(low, INWARD)
        elif kind in "AB":
            name, source, moves = (
                ("second", "first", MIDDLE) if kind == "A" else ("third", "second", OUTWARD)
            )
            (low,) = chain(add_kernel, "add", [shape((2, count, row_len), bf16)], v["part"], v[source])
            v[name] = along_columns(low, moves)
        elif kind == "C":
            v["keep"], *sends, v["own"] = chain(
                functools.partial(curvature_kernel, f),
                "curvature",
                forward + [shape((2, rows, row_len), f32)],
                v["part"],
                v["first"],
                v["second"],
                v["third"],
                own_scales,
                matrices[f],
                scratch=[pltpu.VMEM((2, count, row_len), bf16)],
                flops=flops,
            )
            v["got"] = [swap(send, 0) for send in sends]
        elif kind == "J":
            (low,) = chain(
                bend_half_kernel, "bend_half", [shape((2, count, width), bf16)], v["keep"], *v["got"]
            )
            v["far"] = swap(low, 1)
        elif kind == "K":
            last = n == len(chunks) - 1
            totals[0], v["curvature"], *spread[:] = chain(
                spread_kernel if last else bend_kernel,
                "bend",
                [shape((2, 8, 128), f32), shape((2, count, width), f32)]
                + [shape((TEAM, 128), f32)] * last,
                v["keep"],
                *v["got"],
                v["far"],
                v["own"],
                totals[0],
            )

    for turn in range(max(LAG.values()) + len(chunks)):
        for kind, lag in LAG.items():
            if 0 <= turn - lag < len(chunks):
                step(kind, turn - lag)

    teams = lax.axis_size("freq") // TEAM
    members = [[TEAM * g + d for d in range(TEAM)] for g in range(teams)]
    sums = lax.all_to_all(spread[0], "freq", 0, 0, axis_index_groups=members)
    return chain(
        functools.partial(update_kernel, chunks),
        "update",
        [shape(iterate.shape, f32), shape(spectrum.shape, f32)],
        sums,
        current,
        *(v[name] for name in ("own", "residual", "curvature") for v in values),
    )


def solution(mesh):
    placed = P(("parts", "freq"), None, None, None, None)
    return jax.shard_map(
        body,
        mesh=mesh,
        in_specs=(placed, P("freq", None, None, None, None), P(), placed),
        out_specs=(placed, placed),
        check_vma=False,
    )
```

```python
import functools

import jax
import jax.numpy as jnp
from jax import lax
from jax.experimental import pallas as pl
from jax.experimental.pallas import tpu as pltpu
from jax.sharding import PartitionSpec as P

ROWS = 4
COLS = 4
TEAM = ROWS * COLS
SIZES = ((2, 2), (2, 2))
GROUPS = ((0,), (1,), (2,), (3,))
LAG = {"I": 1, "R": 2, "H": 1, "D": 2, "A": 3, "B": 4, "C": 5, "J": 5, "K": 6}

CORE = 2

f32, bf16 = jnp.float32, jnp.bfloat16
VMEM = pl.BlockSpec(memory_space=pltpu.VMEM)
SMEM = pl.BlockSpec(memory_space=pltpu.SMEM)
ANY = pl.BlockSpec(memory_space=pl.ANY)
HBM = pl.BlockSpec(memory_space=pltpu.HBM)
shape = jax.ShapeDtypeStruct


def team_pairs(pairs):
    groups = lax.axis_size("freq") // TEAM
    return [(TEAM * g + a, TEAM * g + b) for g in range(groups) for a, b in pairs]


def along_columns(value, moves):
    pairs = [(ROWS * a + r, ROWS * b + r) for a, b in moves for r in range(ROWS)]
    return lax.ppermute(value, "freq", team_pairs(pairs))


def swap(value, bit):
    return lax.ppermute(value, "freq", team_pairs([(d, d ^ (1 << bit)) for d in range(TEAM)]))


INWARD = [(0, 1), (3, 2)]
MIDDLE = [(1, 2), (2, 1)]
OUTWARD = [(1, 0), (2, 3)]
SHIFTS = [[(a, (a + k) % COLS) for a in range(COLS)] for k in range(1, COLS)]


def product(left, right):
    return lax.dot_general(left, right, (((1,), (0,)), ((), ())), preferred_element_type=f32)


def product_transposed(left, right):
    return lax.dot_general(left, right, (((1,), (1,)), ((), ())), preferred_element_type=f32)


def slab_of(refs, n):
    each = 4 // len(refs)
    return refs[n // each].at[n % each]


def multiply_columns(core, left, matrix, keep, *sends):
    count = left.shape[0] // 2
    width = keep.shape[3]
    away = [slab_of(sends, n) for n in range(4)]
    for which, outs in ((1 - core, away), (core, [keep.at[n // 2, n % 2] for n in range(4)])):
        for half in range(2):
            real, imag = outs[2 * half : 2 * half + 2]
            cols = pl.ds(pl.multiple_of((2 * half + which) * width, width), width)
            with_real = product(left, matrix[0, :, cols])
            with_imag = product(left, matrix[1, :, cols])
            real[...] = with_real[:count] - with_imag[count:]
            imag[...] = with_imag[:count] + with_real[count:]


def load_kernel(groups, where, matrix_hbm, data_hbm, _, current, scale, *refs):
    freqs = matrix_hbm.shape[0]
    datas, matrices, sems = refs[:freqs], refs[freqs : 2 * freqs], refs[-1]
    pairs = [(data_hbm.at[f], data) for f, data in enumerate(datas)]
    pairs += [(matrix_hbm.at[f], matrix) for f, matrix in enumerate(matrices)]
    copies = [
        pltpu.make_async_copy(source, target, sems.at[n]) for n, (source, target) in enumerate(pairs)
    ]
    for copy in copies:
        copy.start()
    for members, out in zip(groups, refs[2 * freqs : -1]):
        place = 0
        for f, start, size in members:
            for c in range(2):
                rows = current[f, c, start : start + size, :]
                out[c, place : place + size] = (rows * scale[f : f + 1, :]).astype(bf16)
            place += size
    for copy in copies:
        copy.wait()


def image_kernel(start, where, *refs):
    core, col = where[0], where[2]
    fields, (matrix, keep, *sends, left) = refs[:COLS], refs[COLS:]
    for k, field in enumerate(fields):
        left[:, lax.rem(col + COLS - k, COLS)] = field[:, start : start + left.shape[2]]
    rows = 2 * COLS * left.shape[2]
    multiply_columns(core, left[...].reshape(rows, left.shape[3]), matrix, keep, *sends)


def half_kernel(where, keep, *refs):
    *got, low = refs
    for n in range(4):
        low[n // 2, n % 2] = (keep[n // 2, n % 2] + slab_of(got, n)[...]).astype(bf16)


def residual_kernel(start, size, where, keep, *refs):
    *got, far, data, other_data, low, residual = refs
    y = where[1]
    slab = data.shape[1] // COLS
    for half in range(2):
        for source, mine in ((data, True), (other_data, False)):

            @pl.when((y == half) == mine)
            def _(half=half, source=source, mine=mine):
                for c in range(2):
                    for s in range(COLS):
                        rows = pl.ds(s * size, size)
                        image = (keep[half, c, rows] + slab_of(got, 2 * half + c)[rows]) + far[half, c, rows].astype(f32)
                        value = source[c, pl.ds(s * slab + start, size)] - image
                        low[half, c, rows] = value.astype(bf16)
                        if mine:
                            residual[c, rows] = value


def descent_kernel(where, own, other, matrix, low, part, left):
    core = where[0]
    count, width = own.shape[2], own.shape[3]
    for half in range(2):
        for which, ref in ((core, own), (1 - core, other)):
            cols = pl.ds(pl.multiple_of((2 * half + which) * width, width), width)
            left[:, cols] = ref[half].reshape(2 * count, width)
    depth = matrix.shape[1]
    tile = depth // 4
    for k in range(4):
        rows = pl.ds(k * tile, tile)
        with_real = product_transposed(left[...], matrix[0, rows, :])
        with_imag = product_transposed(left[...], matrix[1, rows, :])
        real = with_real[:count] + with_imag[count:]
        imag = with_real[count:] - with_imag[:count]
        part[0, :, rows], part[1, :, rows] = real, imag
        low[0, :, rows], low[1, :, rows] = real.astype(bf16), imag.astype(bf16)


def add_kernel(where, part, got, out):
    out[...] = (part[...] + got[...].astype(f32)).astype(bf16)


def curvature_kernel(f, where, part, first, second, third, scale, matrix, keep, *refs):
    core, col = where[0], where[2]
    *sends, own, left = refs
    count, depth = part.shape[1], part.shape[2]
    piece = own.shape[1]
    row_scale = scale[f : f + 1, :]

    def descent(c, rows):
        inner = part[c, rows] + first[c, rows].astype(f32)
        outer = second[c, rows].astype(f32) + third[c, rows].astype(f32)
        return (inner + outer) * row_scale

    for c in range(2):
        left[c] = (descent(c, pl.ds(0, count)) * row_scale).astype(bf16)
        own[c] = descent(c, pl.ds(pl.multiple_of(col * piece, piece), piece))
    multiply_columns(core, left[...].reshape(2 * count, depth), matrix, keep, *sends)


def bend_half_kernel(where, keep, *refs):
    *got, low = refs
    for half in range(2):

        @pl.when(where[1] != half)
        def _(half=half):
            for c in range(2):
                low[c] = (keep[half, c] + slab_of(got, 2 * half + c)[...]).astype(bf16)


def squares(value):
    return jnp.sum((value * value).reshape(-1, 8, 128), axis=0)


def bend_kernel(where, keep, *refs):
    *got, far, own, sums, out_sums, curvature = refs
    for half in range(2):

        @pl.when(where[1] == half)
        def _(half=half):
            for c in range(2):
                curvature[c] = (keep[half, c] + slab_of(got, 2 * half + c)[...]) + far[c].astype(f32)

    value = curvature[...]
    out_sums[0] = sums[0] + squares(own[...])
    out_sums[1] = sums[1] + squares(value)


def spread_kernel(where, *refs):
    *refs, out = refs
    bend_kernel(where, *refs)
    gamma, bent = (jnp.sum(refs[-2][n], keepdims=True) for n in range(2))
    lane = lax.broadcasted_iota(jnp.int32, out.shape, 1)
    out[...] = jnp.where(lane < out.shape[1] // 2, gamma, bent)


def update_kernel(chunks, where, sums, current, *refs):
    n = len(chunks)
    descents, residuals, curvatures = refs[:n], refs[n : 2 * n], refs[2 * n : 3 * n]
    new_iterate, new_residual = refs[3 * n :]
    total = jnp.sum(sums[...], axis=0, keepdims=True)
    middle = total.shape[1] // 2
    step = total[:, :1] / total[:, middle : middle + 1]
    slab = new_residual.shape[3] // COLS
    for (f, start, size), descent, residual, curvature in zip(
        chunks, descents, residuals, curvatures
    ):
        for c in range(2):
            rows = pl.ds(start, size)
            new_iterate[0, f, c, rows] = current[f, c, rows] + step * descent[c]
            for s in range(COLS):
                rows = pl.ds(s * size, size)
                new_residual[0, f, c, pl.ds(s * slab + start, size)] = (
                    residual[c, rows] - step * curvature[c, rows]
                )


class Chain:
    def __init__(self, where):
        self.where = where
        self.last = None

    def __call__(self, kernel, name, out_shape, *operands, scratch=(), flops=0, specs=None):
        token = [] if self.last is None else [self.last]

        def run(where, *refs):
            return kernel(where, *refs[len(token) :])

        results = pl.pallas_call(
            run,
            in_specs=[SMEM] + [ANY] * len(token) + (specs or [VMEM] * len(operands)),
            out_specs=[VMEM] * len(out_shape),
            out_shape=out_shape,
            scratch_shapes=list(scratch),
            name=name,
            cost_estimate=pl.CostEstimate(
                flops=0, bytes_accessed=1024, transcendentals=0
            ),
            compiler_params=pltpu.CompilerParams(vmem_limit_bytes=32 << 20),
        )(self.where, *token, *operands)
        self.last = results[0]
        return results


def body(spectrum, blocks, scales, iterate):
    index = lax.axis_index("freq")
    where = jnp.stack([index % 2, index // 2 % 2, index // ROWS % COLS, index // TEAM])
    matrix, current, data = blocks[0], iterate[0], spectrum[0]
    freqs, _, row_len, col_len = matrix.shape
    slab, width = current.shape[2], data.shape[3]
    chunks = []
    for f in range(freqs):
        sizes = [slab // 4 * part for part in SIZES[f]]
        chunks += [(f, sum(sizes[:h]), size) for h, size in enumerate(sizes)]
    sent = [[chunks[n] for n in members] for members in GROUPS]
    chain = Chain(where.astype(jnp.int32))

    own_scales = lax.dynamic_slice(
        scales, (index // TEAM * freqs, index % ROWS * row_len), (freqs, row_len)
    )
    f, start, rows = sent[0][0]
    owns = [(current[f, :, start : start + rows] * own_scales[f]).astype(bf16)]
    staged = chain(
        functools.partial(load_kernel, sent[1:]),
        "load",
        [shape(data.shape[1:], f32)] * freqs
        + [shape(matrix.shape[1:], bf16)] * freqs
        + [shape((2, sum(c[2] for c in members), row_len), bf16) for members in sent[1:]],
        matrix,
        data,
        owns[0],
        current,
        own_scales,
        specs=[HBM] * 2 + [ANY] + [VMEM] * 2,
        scratch=[pltpu.SemaphoreType.DMA((2 * freqs,))],
    )
    data, matrices = staged[:freqs], staged[freqs : 2 * freqs]
    owns += staged[2 * freqs :]
    other_data = [swap(rows, 1) for rows in data]
    values = [{} for _ in chunks]
    totals, spread = [jnp.zeros((2, 8, 128), f32)], []

    for members, own in zip(GROUPS, owns):
        gathered = (own, *(along_columns(own, moves) for moves in SHIFTS))
        place = 0
        for n in members:
            values[n]["x"], values[n]["start"] = gathered, place
            place += chunks[n][2]

    def step(kind, n):
        f, start, rows = chunks[n]
        v = values[n]
        count = COLS * rows
        flops = 8 * count * row_len * col_len
        forward = [shape((2, 2, count, width), f32)] + [shape((4 // CORE, count, width), f32)] * CORE
        if kind == "I":
            v["keep"], *sends = chain(
                functools.partial(image_kernel, v["start"]),
                "image",
                forward,
                *v["x"],
                matrices[f],
                scratch=[pltpu.VMEM((2, COLS, rows, row_len), bf16)],
                flops=flops,
            )
            v["got"] = [swap(send, 0) for send in sends]
        elif kind == "H":
            (low,) = chain(half_kernel, "half", [shape((2, 2, count, width), bf16)], v["keep"], *v["got"])
            v["far"] = swap(low, 1)
        elif kind == "R":
            v["low"], v["residual"] = chain(
                functools.partial(residual_kernel, start, rows),
                "residual",
                [shape((2, 2, count, width), bf16), shape((2, count, width), f32)],
                v["keep"],
                *v["got"],
                v["far"],
                data[f],
                other_data[f],
            )
            v["other_low"] = swap(v["low"], 0)
        elif kind == "D":
            low, v["part"] = chain(
                descent_kernel,
                "descent",
                [shape((2, count, row_len), bf16), shape((2, count, row_len), f32)],
                v["low"],
                v["other_low"],
                matrices[f],
                scratch=[pltpu.VMEM((2 * count, col_len), bf16)],
                flops=flops,
            )
            v["first"] = along_columns(low, INWARD)
        elif kind in "AB":
            name, source, moves = (
                ("second", "first", MIDDLE) if kind == "A" else ("third", "second", OUTWARD)
            )
            (low,) = chain(add_kernel, "add", [shape((2, count, row_len), bf16)], v["part"], v[source])
            v[name] = along_columns(low, moves)
        elif kind == "C":
            v["keep"], *sends, v["own"] = chain(
                functools.partial(curvature_kernel, f),
                "curvature",
                forward + [shape((2, rows, row_len), f32)],
                v["part"],
                v["first"],
                v["second"],
                v["third"],
                own_scales,
                matrices[f],
                scratch=[pltpu.VMEM((2, count, row_len), bf16)],
                flops=flops,
            )
            v["got"] = [swap(send, 0) for send in sends]
        elif kind == "J":
            (low,) = chain(
                bend_half_kernel, "bend_half", [shape((2, count, width), bf16)], v["keep"], *v["got"]
            )
            v["far"] = swap(low, 1)
        elif kind == "K":
            last = n == len(chunks) - 1
            totals[0], v["curvature"], *spread[:] = chain(
                spread_kernel if last else bend_kernel,
                "bend",
                [shape((2, 8, 128), f32), shape((2, count, width), f32)]
                + [shape((TEAM, 128), f32)] * last,
                v["keep"],
                *v["got"],
                v["far"],
                v["own"],
                totals[0],
            )

    for turn in range(max(LAG.values()) + len(chunks)):
        for kind, lag in LAG.items():
            if 0 <= turn - lag < len(chunks):
                step(kind, turn - lag)

    teams = lax.axis_size("freq") // TEAM
    members = [[TEAM * g + d for d in range(TEAM)] for g in range(teams)]
    sums = lax.all_to_all(spread[0], "freq", 0, 0, axis_index_groups=members)
    return chain(
        functools.partial(update_kernel, chunks),
        "update",
        [shape(iterate.shape, f32), shape(spectrum.shape, f32)],
        sums,
        current,
        *(v[name] for name in ("own", "residual", "curvature") for v in values),
    )


def solution(mesh):
    placed = P(("parts", "freq"), None, None, None, None)
    return jax.shard_map(
        body,
        mesh=mesh,
        in_specs=(placed, P("freq", None, None, None, None), P(), placed),
        out_specs=(placed, placed),
        check_vma=False,
    )
```

```python
import functools

import jax
import jax.numpy as jnp
from jax import lax
from jax.experimental import pallas as pl
from jax.experimental.pallas import tpu as pltpu
from jax.sharding import PartitionSpec as P

ROWS = 4
COLS = 4
TEAM = ROWS * COLS
SIZES = ((2, 2), (2, 2))
GROUPS = ((0,), (1,), (2,), (3,))
LAG = {"I": 1, "R": 2, "H": 1, "D": 2, "A": 3, "B": 4, "C": 5, "J": 5, "K": 6}

CORE = 2

f32, bf16 = jnp.float32, jnp.bfloat16
VMEM = pl.BlockSpec(memory_space=pltpu.VMEM)
SMEM = pl.BlockSpec(memory_space=pltpu.SMEM)
ANY = pl.BlockSpec(memory_space=pl.ANY)
HBM = pl.BlockSpec(memory_space=pltpu.HBM)
shape = jax.ShapeDtypeStruct


def team_pairs(pairs):
    groups = lax.axis_size("freq") // TEAM
    return [(TEAM * g + a, TEAM * g + b) for g in range(groups) for a, b in pairs]


def along_columns(value, moves):
    pairs = [(ROWS * a + r, ROWS * b + r) for a, b in moves for r in range(ROWS)]
    return lax.ppermute(value, "freq", team_pairs(pairs))


def swap(value, bit):
    return lax.ppermute(value, "freq", team_pairs([(d, d ^ (1 << bit)) for d in range(TEAM)]))


INWARD = [(0, 1), (3, 2)]
MIDDLE = [(1, 2), (2, 1)]
OUTWARD = [(1, 0), (2, 3)]
SHIFTS = [[(a, (a + k) % COLS) for a in range(COLS)] for k in range(1, COLS)]


def product(left, right):
    return lax.dot_general(left, right, (((1,), (0,)), ((), ())), preferred_element_type=f32)


def product_transposed(left, right):
    return lax.dot_general(left, right, (((1,), (1,)), ((), ())), preferred_element_type=f32)


def slab_of(refs, n):
    each = 4 // len(refs)
    return refs[n // each].at[n % each]


def multiply_columns(core, left, matrix, keep, *sends):
    count = left.shape[0] // 2
    width = keep.shape[3]
    away = [slab_of(sends, n) for n in range(4)]
    for which, outs in ((1 - core, away), (core, [keep.at[n // 2, n % 2] for n in range(4)])):
        for half in range(2):
            real, imag = outs[2 * half : 2 * half + 2]
            cols = pl.ds(pl.multiple_of((2 * half + which) * width, width), width)
            with_real = product(left, matrix[0, :, cols])
            with_imag = product(left, matrix[1, :, cols])
            real[...] = with_real[:count] - with_imag[count:]
            imag[...] = with_imag[:count] + with_real[count:]


def load_kernel(groups, where, matrix_hbm, data_hbm, _, current, scale, *refs):
    freqs = matrix_hbm.shape[0]
    datas, matrices, sems = refs[:freqs], refs[freqs : 2 * freqs], refs[-1]
    pairs = [(data_hbm.at[f], data) for f, data in enumerate(datas)]
    pairs += [(matrix_hbm.at[f], matrix) for f, matrix in enumerate(matrices)]
    copies = [
        pltpu.make_async_copy(source, target, sems.at[n]) for n, (source, target) in enumerate(pairs)
    ]
    for copy in copies:
        copy.start()
    for members, out in zip(groups, refs[2 * freqs : -1]):
        place = 0
        for f, start, size in members:
            for c in range(2):
                rows = current[f, c, start : start + size, :]
                out[c, place : place + size] = (rows * scale[f : f + 1, :]).astype(bf16)
            place += size
    for copy in copies:
        copy.wait()


def image_kernel(start, where, *refs):
    core, col = where[0], where[2]
    fields, (matrix, keep, *sends, left) = refs[:COLS], refs[COLS:]
    for k, field in enumerate(fields):
        left[:, lax.rem(col + COLS - k, COLS)] = field[:, start : start + left.shape[2]]
    rows = 2 * COLS * left.shape[2]
    multiply_columns(core, left[...].reshape(rows, left.shape[3]), matrix, keep, *sends)


def half_kernel(where, keep, *refs):
    *got, low = refs
    for n in range(4):
        low[n // 2, n % 2] = (keep[n // 2, n % 2] + slab_of(got, n)[...]).astype(bf16)


def residual_kernel(start, size, where, keep, *refs):
    *got, far, data, other_data, low, residual = refs
    y = where[1]
    slab = data.shape[1] // COLS
    for half in range(2):
        for source, mine in ((data, True), (other_data, False)):

            @pl.when((y == half) == mine)
            def _(half=half, source=source, mine=mine):
                for c in range(2):
                    for s in range(COLS):
                        rows = pl.ds(s * size, size)
                        image = (keep[half, c, rows] + slab_of(got, 2 * half + c)[rows]) + far[half, c, rows].astype(f32)
                        value = source[c, pl.ds(s * slab + start, size)] - image
                        low[half, c, rows] = value.astype(bf16)
                        if mine:
                            residual[c, rows] = value


def descent_kernel(where, own, other, matrix, low, part, left):
    core = where[0]
    count, width = own.shape[2], own.shape[3]
    for half in range(2):
        for which, ref in ((core, own), (1 - core, other)):
            cols = pl.ds(pl.multiple_of((2 * half + which) * width, width), width)
            left[:, cols] = ref[half].reshape(2 * count, width)
    depth = matrix.shape[1]
    tile = depth // 4
    for k in range(4):
        rows = pl.ds(k * tile, tile)
        with_real = product_transposed(left[...], matrix[0, rows, :])
        with_imag = product_transposed(left[...], matrix[1, rows, :])
        real = with_real[:count] + with_imag[count:]
        imag = with_real[count:] - with_imag[:count]
        part[0, :, rows], part[1, :, rows] = real, imag
        low[0, :, rows], low[1, :, rows] = real.astype(bf16), imag.astype(bf16)


def add_kernel(where, part, got, out):
    out[...] = (part[...] + got[...].astype(f32)).astype(bf16)


def curvature_kernel(f, where, part, first, second, third, scale, matrix, keep, *refs):
    core, col = where[0], where[2]
    *sends, own, left = refs
    count, depth = part.shape[1], part.shape[2]
    piece = own.shape[1]
    row_scale = scale[f : f + 1, :]

    def descent(c, rows):
        inner = part[c, rows] + first[c, rows].astype(f32)
        outer = second[c, rows].astype(f32) + third[c, rows].astype(f32)
        return (inner + outer) * row_scale

    for c in range(2):
        left[c] = (descent(c, pl.ds(0, count)) * row_scale).astype(bf16)
        own[c] = descent(c, pl.ds(pl.multiple_of(col * piece, piece), piece))
    multiply_columns(core, left[...].reshape(2 * count, depth), matrix, keep, *sends)


def bend_half_kernel(where, keep, *refs):
    *got, low = refs
    for half in range(2):

        @pl.when(where[1] != half)
        def _(half=half):
            for c in range(2):
                low[c] = (keep[half, c] + slab_of(got, 2 * half + c)[...]).astype(bf16)


def squares(value):
    return jnp.sum((value * value).reshape(-1, 8, 128), axis=0)


def bend_kernel(where, keep, *refs):
    *got, far, own, sums, out_sums, curvature = refs
    for half in range(2):

        @pl.when(where[1] == half)
        def _(half=half):
            for c in range(2):
                curvature[c] = (keep[half, c] + slab_of(got, 2 * half + c)[...]) + far[c].astype(f32)

    value = curvature[...]
    out_sums[0] = sums[0] + squares(own[...])
    out_sums[1] = sums[1] + squares(value)


def spread_kernel(where, *refs):
    *refs, out = refs
    bend_kernel(where, *refs)
    gamma, bent = (jnp.sum(refs[-2][n], keepdims=True) for n in range(2))
    lane = lax.broadcasted_iota(jnp.int32, out.shape, 1)
    out[...] = jnp.where(lane < out.shape[1] // 2, gamma, bent)


def update_kernel(chunks, where, sums, current, *refs):
    n = len(chunks)
    descents, residuals, curvatures = refs[:n], refs[n : 2 * n], refs[2 * n : 3 * n]
    *results, new_iterate, new_residual, sems = refs[3 * n :]
    copies = []
    total = jnp.sum(sums[...], axis=0, keepdims=True)
    middle = total.shape[1] // 2
    step = total[:, :1] / total[:, middle : middle + 1]
    slab = new_residual.shape[3] // COLS
    for (f, start, size), descent, residual, curvature in zip(
        chunks, descents, residuals, curvatures
    ):
        for c in range(2):
            rows = pl.ds(start, size)
            new_iterate[0, f, c, rows] = current[f, c, rows] + step * descent[c]
            for s in range(COLS):
                rows = pl.ds(s * size, size)
                new_residual[0, f, c, pl.ds(s * slab + start, size)] = (
                    residual[c, rows] - step * curvature[c, rows]
                )
        if start + size == current.shape[2]:
            for k, (source, target) in enumerate(zip((new_iterate, new_residual), results)):
                copy = pltpu.make_async_copy(source.at[0, f], target.at[0, f], sems.at[2 * f + k])
                copy.start()
                copies.append(copy)
    for copy in copies:
        copy.wait()


class Chain:
    def __init__(self, where):
        self.where = where
        self.last = None

    def __call__(self, kernel, name, out_shape, *operands, scratch=(), flops=0, specs=None, out=VMEM):
        token = [] if self.last is None else [self.last]

        def run(where, *refs):
            return kernel(where, *refs[len(token) :])

        results = pl.pallas_call(
            run,
            in_specs=[SMEM] + [ANY] * len(token) + (specs or [VMEM] * len(operands)),
            out_specs=[out] * len(out_shape),
            out_shape=out_shape,
            scratch_shapes=list(scratch),
            name=name,
            cost_estimate=pl.CostEstimate(
                flops=0, bytes_accessed=1024, transcendentals=0
            ),
            compiler_params=pltpu.CompilerParams(vmem_limit_bytes=32 << 20),
        )(self.where, *token, *operands)
        self.last = results[0]
        return results


def body(spectrum, blocks, scales, iterate):
    index = lax.axis_index("freq")
    where = jnp.stack([index % 2, index // 2 % 2, index // ROWS % COLS, index // TEAM])
    matrix, current, data = blocks[0], iterate[0], spectrum[0]
    freqs, _, row_len, col_len = matrix.shape
    slab, width = current.shape[2], data.shape[3]
    chunks = []
    for f in range(freqs):
        sizes = [slab // 4 * part for part in SIZES[f]]
        chunks += [(f, sum(sizes[:h]), size) for h, size in enumerate(sizes)]
    sent = [[chunks[n] for n in members] for members in GROUPS]
    chain = Chain(where.astype(jnp.int32))

    own_scales = lax.dynamic_slice(
        scales, (index // TEAM * freqs, index % ROWS * row_len), (freqs, row_len)
    )
    f, start, rows = sent[0][0]
    owns = [(current[f, :, start : start + rows] * own_scales[f]).astype(bf16)]
    staged = chain(
        functools.partial(load_kernel, sent[1:]),
        "load",
        [shape(data.shape[1:], f32)] * freqs
        + [shape(matrix.shape[1:], bf16)] * freqs
        + [shape((2, sum(c[2] for c in members), row_len), bf16) for members in sent[1:]],
        matrix,
        data,
        owns[0],
        current,
        own_scales,
        specs=[HBM] * 2 + [ANY] + [VMEM] * 2,
        scratch=[pltpu.SemaphoreType.DMA((2 * freqs,))],
    )
    data, matrices = staged[:freqs], staged[freqs : 2 * freqs]
    owns += staged[2 * freqs :]
    other_data = [swap(rows, 1) for rows in data]
    values = [{} for _ in chunks]
    totals, spread = [jnp.zeros((2, 8, 128), f32)], []

    for members, own in zip(GROUPS, owns):
        gathered = (own, *(along_columns(own, moves) for moves in SHIFTS))
        place = 0
        for n in members:
            values[n]["x"], values[n]["start"] = gathered, place
            place += chunks[n][2]

    def step(kind, n):
        f, start, rows = chunks[n]
        v = values[n]
        count = COLS * rows
        flops = 8 * count * row_len * col_len
        forward = [shape((2, 2, count, width), f32)] + [shape((4 // CORE, count, width), f32)] * CORE
        if kind == "I":
            v["keep"], *sends = chain(
                functools.partial(image_kernel, v["start"]),
                "image",
                forward,
                *v["x"],
                matrices[f],
                scratch=[pltpu.VMEM((2, COLS, rows, row_len), bf16)],
                flops=flops,
            )
            v["got"] = [swap(send, 0) for send in sends]
        elif kind == "H":
            (low,) = chain(half_kernel, "half", [shape((2, 2, count, width), bf16)], v["keep"], *v["got"])
            v["far"] = swap(low, 1)
        elif kind == "R":
            v["low"], v["residual"] = chain(
                functools.partial(residual_kernel, start, rows),
                "residual",
                [shape((2, 2, count, width), bf16), shape((2, count, width), f32)],
                v["keep"],
                *v["got"],
                v["far"],
                data[f],
                other_data[f],
            )
            v["other_low"] = swap(v["low"], 0)
        elif kind == "D":
            low, v["part"] = chain(
                descent_kernel,
                "descent",
                [shape((2, count, row_len), bf16), shape((2, count, row_len), f32)],
                v["low"],
                v["other_low"],
                matrices[f],
                scratch=[pltpu.VMEM((2 * count, col_len), bf16)],
                flops=flops,
            )
            v["first"] = along_columns(low, INWARD)
        elif kind in "AB":
            name, source, moves = (
                ("second", "first", MIDDLE) if kind == "A" else ("third", "second", OUTWARD)
            )
            (low,) = chain(add_kernel, "add", [shape((2, count, row_len), bf16)], v["part"], v[source])
            v[name] = along_columns(low, moves)
        elif kind == "C":
            v["keep"], *sends, v["own"] = chain(
                functools.partial(curvature_kernel, f),
                "curvature",
                forward + [shape((2, rows, row_len), f32)],
                v["part"],
                v["first"],
                v["second"],
                v["third"],
                own_scales,
                matrices[f],
                scratch=[pltpu.VMEM((2, count, row_len), bf16)],
                flops=flops,
            )
            v["got"] = [swap(send, 0) for send in sends]
        elif kind == "J":
            (low,) = chain(
                bend_half_kernel, "bend_half", [shape((2, count, width), bf16)], v["keep"], *v["got"]
            )
            v["far"] = swap(low, 1)
        elif kind == "K":
            last = n == len(chunks) - 1
            totals[0], v["curvature"], *spread[:] = chain(
                spread_kernel if last else bend_kernel,
                "bend",
                [shape((2, 8, 128), f32), shape((2, count, width), f32)]
                + [shape((TEAM, 128), f32)] * last,
                v["keep"],
                *v["got"],
                v["far"],
                v["own"],
                totals[0],
            )

    for turn in range(max(LAG.values()) + len(chunks)):
        for kind, lag in LAG.items():
            if 0 <= turn - lag < len(chunks):
                step(kind, turn - lag)

    teams = lax.axis_size("freq") // TEAM
    members = [[TEAM * g + d for d in range(TEAM)] for g in range(teams)]
    sums = lax.all_to_all(spread[0], "freq", 0, 0, axis_index_groups=members)
    return chain(
        functools.partial(update_kernel, chunks),
        "update",
        [shape(iterate.shape, f32), shape(spectrum.shape, f32)],
        sums,
        current,
        *(v[name] for name in ("own", "residual", "curvature") for v in values),
        out=HBM,
        scratch=[
            pltpu.VMEM(iterate.shape, f32),
            pltpu.VMEM(spectrum.shape, f32),
            pltpu.SemaphoreType.DMA((2 * freqs,)),
        ],
    )


def solution(mesh):
    placed = P(("parts", "freq"), None, None, None, None)
    return jax.shard_map(
        body,
        mesh=mesh,
        in_specs=(placed, P("freq", None, None, None, None), P(), placed),
        out_specs=(placed, placed),
        check_vma=False,
    )
```
